32 devices in a mesh: groups: 2 (over y), dp: 4 (over z), tensor: 2 (over x), pipe: 2 (over core).
Axes of the slice: x: 2, y: 2, z: 4, core: 2. Of those that a mesh axis runs over, the one named last changes fastest.
Arguments:
- acts: bfloat16 [8192, 8192], P(('groups', 'dp'), ('tensor', 'pipe')), parts along dimension 0, may hold values from -6 to 6
- frozen_value_weight: bfloat16 [8192, 1024], P(('tensor', 'pipe'), 'dp'), may hold values from -0.0625 to 0.0625
- adapter_down_maps: bfloat16 [16, 8192, 64], P('dp', ('tensor', 'pipe')), may hold values from -0.0625 to 0.0625
- adapter_up_maps: bfloat16 [16, 64, 1024], P('dp', None, ('tensor', 'pipe')), may hold values from -0.75 to 0.75
- output_gradient: bfloat16 [8192, 1024], P(('groups', 'dp'), ('tensor', 'pipe')), parts along dimension 0, may hold values from -6 to 6
- token_adapter: int32 [8192, 1], P(('groups', 'dp')), parts along dimension 0, may hold values from 0 to 15; in each aligned block of 1024 rows (0 to 1023, 1024 to 2047, ...) at most 96 rows name the same one
- adapter_slot: int32 [16], replicated, may hold values from 0 to 15, each once
Outputs:
- layer_out: bfloat16 [8192, 1024], P(('groups', 'dp'), ('tensor', 'pipe')), parts along dimension 0
- input_gradient: bfloat16 [8192, 8192], P(('groups', 'dp'), ('tensor', 'pipe')), parts along dimension 0
- grad_down: float32 [32, 8192, 64], P(('groups', 'dp'), ('tensor', 'pipe')), parts along dimension 0
- grad_up: float32 [32, 64, 1024], P(('groups', 'dp'), None, ('tensor', 'pipe')), parts along dimension 0
The draws below stay inside these ranges and needn't reach their ends.
There are 2 independent parts, one for each index of `groups`. The reference program is written for one: setup_inputs(seed, part) draws one part's arguments, and reference() takes and returns one part's arrays. A program takes and returns all parts, laid end to end along the dimension named above; an argument that names none is the same for every part. Nothing has to cross between parts.
Inputs may be any that keep to these rules, and one draw needn't show every extreme that they name: `token_adapter`: within the rows of one device (aligned blocks of 1024 rows) no adapter is named by more than 96 rows, a bound that some block reaches; every adapter is named by some row. Each slot once; adapter a's maps lie at slot adapter_slot[a], which index dp number adapter_slot[a] // 4 holds.
All inputs are finite; a program needn't handle non-finite values.
Results may differ from the reference program's by a relative error of at most 0.015.
Values may be sent and summed in bfloat16 or wider, within the bound.
A program may use at most 128 MiB of HBM per device.

```python
import math
import jax
import jax.numpy as jnp
import numpy as np
from jax import lax

MODEL_WIDTH = 8192
VALUE_WIDTH = 1024
ADAPTER_RANK = 64
TOK_DEV = 1024
ADAPTER_TOTAL = 16
MOST = 96
TOKENS = 4096
N_DP = 4
N_TENSOR = 2
N_PIPE = 2


def level_of(rng, extent, split, low, high):
    level = 1.0
    for dim, blocks in split:
        draws = jax.random.uniform(jax.random.fold_in(jax.random.fold_in(rng, 6), dim), (blocks,), jnp.float32, low / len(split), high / len(split))
        level = level * jnp.repeat(jnp.exp(draws), extent[dim] // blocks).reshape((-1,) + (1,) * (len(extent) - 1 - dim))
    return level


def routed_block(rng, own, number, rows, count, top, bound, slope):
    order = jax.random.permutation(rng, count)
    crowded, usual = load_shares(count, rows * top, bound, slope, True), load_shares(count, rows * top, bound, slope, False)
    places = jnp.arange(count)

    def named(lengths, rotation):
        used = int((lengths > 0).sum())
        fixed = max(1, used // 4)
        shifted = fixed + (places - fixed + rotation * (used - fixed)) % max(1, count - fixed)
        return jnp.zeros((count,), jnp.int32).at[order[jnp.where(places < fixed, places, shifted)]].set(jnp.asarray(lengths, jnp.int32))

    lengths = jnp.where(number % 4 == 0, named(crowded, number // 4), named(usual, number - number // 4 - 1))
    mixed = jax.random.permutation(jax.random.fold_in(own, 3), count)
    giver, sink = mixed[0:count // 2 * 2:2], mixed[1:count // 2 * 2:2]
    margin = jnp.minimum(lengths[giver] - 1, bound - lengths[sink]) // 2
    margin = jnp.where((giver == order[0]) | (sink == order[0]) | (lengths[sink] == 0), 0, jnp.maximum(margin, 0))
    shifted = jax.random.randint(jax.random.fold_in(own, 4), (count // 2,), 0, 1 << 20) % (margin + 1)
    lengths = lengths.at[giver].add(-shifted).at[sink].add(shifted)
    items = jnp.searchsorted(jnp.cumsum(lengths), jnp.arange(rows * top), side="right").astype(jnp.int32)
    grid = items.reshape(top, rows).T
    grid = grid[jax.random.permutation(jax.random.fold_in(own, 1), rows)]
    rotation = jax.random.randint(jax.random.fold_in(own, 2), (rows, 1), 0, top)
    return jnp.take_along_axis(grid, (jnp.arange(top)[None, :] + rotation) % top, axis=1)


def load_shares(count, total, reach, slope, full):
    loads = [(1 << 20) // math.isqrt(grade ** slope) + 1 for grade in range(1, count + 1)]
    largest = reach if full else min(reach, max(-(-total // count), total * loads[0] // sum(loads)))
    least = 1 if total - largest >= count - 1 else 0
    given, surplus = [largest] + [least] * (count - 1), total - largest - least * (count - 1)
    while surplus > 0:
        candidates = [i for i in range(1, count) if given[i] < largest] or [i for i in range(1, count) if given[i] < reach]
        pool, remaining = sum([loads[i] for i in candidates]), surplus
        for i in candidates:
            addition = min(reach - given[i], max(1, remaining * loads[i] // pool), surplus)
            given[i] = given[i] + addition
            surplus = surplus - addition
    return np.array(given)


def bell_draw(key, dims, deviation, limit, shards=(), kind=jnp.bfloat16):
    values = deviation * jax.random.normal(key, dims, jnp.float32)
    if shards:
        values = values * level_of(key, dims, shards, -0.22, 0.18)
    return jnp.clip(values, -limit, limit).astype(kind)


def setup_inputs(seed: int = 0, part: int = 0) -> dict:
    streams_of = jax.random.split(jax.random.key(seed), 8)
    own_keys = jax.random.split(jax.random.fold_in(streams_of[7], part), 8)
    acts = bell_draw(own_keys[0], (TOKENS, MODEL_WIDTH), 1.0, 6.0, ((0, 4), (1, 4)))
    frozen_value_weight = bell_draw(streams_of[1], (MODEL_WIDTH, VALUE_WIDTH), MODEL_WIDTH ** -0.5, 0.0625, ((0, 4), (1, 4)))
    adapter_down_maps = bell_draw(streams_of[2], (ADAPTER_TOTAL, MODEL_WIDTH, ADAPTER_RANK), MODEL_WIDTH ** -0.5, 0.0625, ((0, 4), (1, 4)))
    adapter_up_maps = bell_draw(streams_of[3], (ADAPTER_TOTAL, ADAPTER_RANK, VALUE_WIDTH), ADAPTER_RANK ** -0.5, 0.75, ((0, 4), (2, 4)))
    output_gradient = bell_draw(own_keys[4], (TOKENS, VALUE_WIDTH), 1.0, 6.0, ((0, 4), (1, 4)))
    token_adapter_keys = jax.random.split(jax.random.fold_in(own_keys[5], 1), TOKENS // TOK_DEV)
    token_adapter_turns = jax.random.permutation(jax.random.fold_in(own_keys[5], 3), TOKENS // TOK_DEV)
    token_adapter = jax.vmap(lambda own, number: routed_block(jax.random.fold_in(own_keys[5], 2), own, number, TOK_DEV, ADAPTER_TOTAL, 1, MOST, 2))(token_adapter_keys, token_adapter_turns).reshape((TOKENS, 1))
    adapter_slot = jax.random.permutation(streams_of[6], ADAPTER_TOTAL).astype(jnp.int32)
    return {"acts": acts, "frozen_value_weight": frozen_value_weight, "adapter_down_maps": adapter_down_maps, "adapter_up_maps": adapter_up_maps, "output_gradient": output_gradient, "token_adapter": token_adapter, "adapter_slot": adapter_slot}


adapter_scale = 2.0


def reference(acts, frozen_value_weight, adapter_down_maps, adapter_up_maps, output_gradient, token_adapter, adapter_slot):
    blocks = N_TENSOR * N_PIPE
    feat_width = MODEL_WIDTH // blocks
    token_ids = token_adapter[:, 0]
    everyone = jnp.arange(ADAPTER_TOTAL, dtype=jnp.int32)
    chosen = (token_ids[:, None] == everyone[None, :]).astype(jnp.int32)
    slot_tok = jnp.sum(chosen * adapter_slot[None, :], axis=1)
    per_device = chosen.reshape(N_DP, TOK_DEV, ADAPTER_TOTAL)
    before = jnp.sum((jnp.cumsum(per_device, axis=1) - per_device) * per_device, axis=2).reshape(TOKENS)
    source = jnp.arange(TOKENS, dtype=jnp.int32) // TOK_DEV
    flat_pos = slot_tok * (N_DP * MOST) + source * MOST + before
    slot_lookup = jnp.full((ADAPTER_TOTAL * N_DP * MOST,), TOKENS, dtype=jnp.int32)
    slot_lookup = slot_lookup.at[flat_pos].set(jnp.arange(TOKENS, dtype=jnp.int32)).reshape(ADAPTER_TOTAL, N_DP * MOST)
    id_counts = jnp.sum(chosen, axis=0).astype(jnp.float32)
    count_per_slot = jnp.sum((adapter_slot[None, :] == everyone[:, None]).astype(jnp.float32) * id_counts[None, :], axis=1)
    padded_x = jnp.concatenate([acts, jnp.zeros((1, MODEL_WIDTH), acts.dtype)], axis=0)
    padded_dy = jnp.concatenate([output_gradient, jnp.zeros((1, VALUE_WIDTH), output_gradient.dtype)], axis=0)

    def slot_grouped(carry, inputs):
        token_delta_rows, token_back_grad = carry
        lookup_row, down_matrix, up_matrix, token_counts = inputs
        token_rows = padded_x[lookup_row]
        gradient_row_block = padded_dy[lookup_row]
        lowrank = jnp.dot(token_rows, down_matrix, preferred_element_type=jnp.float32)
        rank_space_rows = lowrank.astype(jnp.bfloat16)
        adapter_delta = (adapter_scale * jnp.dot(rank_space_rows, up_matrix, preferred_element_type=jnp.float32)).astype(jnp.bfloat16)
        rank_space_gradient = (adapter_scale * jnp.dot(gradient_row_block, up_matrix.T, preferred_element_type=jnp.float32)).astype(jnp.bfloat16)
        adapter_back_grad = jnp.dot(rank_space_gradient, down_matrix.T, preferred_element_type=jnp.float32).astype(jnp.bfloat16)
        grad_a = jnp.dot(token_rows.T, rank_space_gradient, preferred_element_type=jnp.float32) * (1.0 / token_counts)
        up_map_gradient = jnp.dot(rank_space_rows.T, gradient_row_block, preferred_element_type=jnp.float32) * (adapter_scale / token_counts)
        token_delta_rows = token_delta_rows.at[lookup_row].set(adapter_delta)
        token_back_grad = token_back_grad.at[lookup_row].set(adapter_back_grad)
        return (token_delta_rows, token_back_grad), (grad_a, up_map_gradient)

    initial_state = (jnp.zeros((TOKENS + 1, VALUE_WIDTH), jnp.bfloat16), jnp.zeros((TOKENS + 1, MODEL_WIDTH), jnp.bfloat16))
    (token_delta_rows, token_back_grad), (grad_down, grad_up) = lax.scan(
        slot_grouped, initial_state, (slot_lookup, adapter_down_maps, adapter_up_maps, count_per_slot))

    def base_block(running, block_index):
        act_block = lax.dynamic_slice_in_dim(acts, block_index * feat_width, feat_width, 1)
        weight_block = lax.dynamic_slice_in_dim(frozen_value_weight, block_index * feat_width, feat_width, 0)
        partial_value = jnp.dot(act_block, weight_block, preferred_element_type=jnp.float32).astype(jnp.bfloat16)
        return running + lax.optimization_barrier(partial_value).astype(jnp.float32), None

    base_out, _ = lax.scan(base_block, jnp.zeros((TOKENS, VALUE_WIDTH), jnp.float32), jnp.arange(blocks, dtype=jnp.int32))
    layer_out = (base_out + token_delta_rows[:TOKENS].astype(jnp.float32)).astype(jnp.bfloat16)
    frozen_back_grad = lax.dot_general(output_gradient, frozen_value_weight, (((1,), (1,)), ((), ())), preferred_element_type=jnp.float32)
    input_gradient = (frozen_back_grad + token_back_grad[:TOKENS].astype(jnp.float32)).astype(jnp.bfloat16)
    return layer_out, input_gradient, grad_down, grad_up
```

```python
import jax
import jax.numpy as jnp
from jax import lax
from jax.sharding import PartitionSpec as P

adapter_scale = 2.0
TP = ("tensor", "pipe")


def dot(a, b, dims):
    return lax.dot_general(a, b, (dims, ((), ())), preferred_element_type=jnp.float32)


def local(acts, weight, down, up, dy, token_adapter, adapter_slot):
    per, feat, rank = down.shape
    cols = up.shape[2]
    tok = acts.shape[0]
    adapters = adapter_slot.shape[0]
    wide = adapters * rank
    fold = 2 * rank
    ids = token_adapter[:, 0]
    chosen = ids[:, None] == jnp.arange(adapters, dtype=jnp.int32)[None, :]
    slot_tok = jnp.sum(jnp.where(chosen, adapter_slot[None, :], 0), axis=1)
    slot_hot = slot_tok[:, None] == jnp.arange(adapters, dtype=jnp.int32)[None, :]
    counts = lax.psum(jnp.sum(slot_hot.astype(jnp.float32), axis=0), "dp")
    first = lax.axis_index("dp") * per
    own_counts = lax.dynamic_slice(counts, (first,), (per,))
    mask = slot_tok[:, None] == jnp.arange(wide, dtype=jnp.int32)[None, :] // rank

    def squeeze(full):
        full = jnp.where(mask, full, 0.0)
        return sum(full[:, i : i + fold] for i in range(0, wide, fold))

    def spread(rows):
        return jnp.where(mask, jnp.tile(rows, (1, wide // fold)), 0).astype(jnp.bfloat16)

    up_all = lax.all_gather(up.reshape(per * rank, cols), "dp", axis=0, tiled=True)
    down_all = lax.all_gather(
        down.transpose(1, 0, 2).reshape(feat, per * rank), "dp", axis=1, tiled=True
    )
    weight_all = lax.all_gather(weight, "dp", axis=1, tiled=True)
    dy_all = lax.all_gather(dy, TP, axis=1, tiled=True)

    grad_low = squeeze(dot(dy, up_all, ((1,), (1,)))).astype(jnp.bfloat16)
    grad_low = lax.psum(grad_low, TP).astype(jnp.float32) * adapter_scale
    grad_low = spread(grad_low.astype(jnp.bfloat16))
    part_down = dot(grad_low, acts, ((0,), (0,))).astype(jnp.bfloat16)
    sum_down = lax.psum_scatter(part_down, "dp", scatter_dimension=0, tiled=True)

    low = squeeze(dot(acts, down_all, ((1,), (0,)))).astype(jnp.bfloat16)
    low = spread(lax.psum(low, TP))
    part_up = dot(low, dy, ((0,), (0,))).astype(jnp.bfloat16)
    sum_up = lax.psum_scatter(part_up, "dp", scatter_dimension=0, tiled=True)
    delta = adapter_scale * dot(low, up_all, ((1,), (0,)))

    base = dot(acts, weight_all, ((1,), (0,))).astype(jnp.bfloat16)
    base = lax.psum_scatter(base, TP, scatter_dimension=1, tiled=True)
    layer_out = (base.astype(jnp.float32) + delta).astype(jnp.bfloat16)
    input_gradient = (
        dot(dy_all, weight_all, ((1,), (1,))) + dot(grad_low, down_all, ((1,), (1,)))
    ).astype(jnp.bfloat16)
    grad_down = sum_down.astype(jnp.float32).reshape(per, rank, feat).transpose(0, 2, 1)
    grad_down = grad_down * (1.0 / own_counts)[:, None, None]
    grad_up = sum_up.astype(jnp.float32).reshape(per, rank, cols)
    grad_up = grad_up * (adapter_scale / own_counts)[:, None, None]
    return (layer_out, input_gradient, grad_down, grad_up)


def solution(mesh):
    return jax.shard_map(
        local,
        mesh=mesh,
        in_specs=(
            P(("groups", "dp"), TP),
            P(TP, "dp"),
            P("dp", TP, None),
            P("dp", None, TP),
            P(("groups", "dp"), TP),
            P(("groups", "dp"), None),
            P(),
        ),
        out_specs=(
            P(("groups", "dp"), TP),
            P(("groups", "dp"), TP),
            P(("groups", "dp"), TP, None),
            P(("groups", "dp"), None, TP),
        ),
        check_vma=False,
    )
```

```python
import functools

import jax
import jax.numpy as jnp
from jax import lax
from jax.experimental import pallas as pl
from jax.experimental.pallas import tpu as pltpu
from jax.sharding import PartitionSpec as P

adapter_scale = 2.0
TP = ("tensor", "pipe")


def dot(a, b, dims):
    return lax.dot_general(a, b, (dims, ((), ())), preferred_element_type=jnp.float32)


def plain(acts, weight, down, up, dy, token_adapter, adapter_slot):
    per, feat, rank = down.shape
    cols = up.shape[2]
    tok = acts.shape[0]
    adapters = adapter_slot.shape[0]
    wide = adapters * rank
    fold = 2 * rank
    ids = token_adapter[:, 0]
    chosen = ids[:, None] == jnp.arange(adapters, dtype=jnp.int32)[None, :]
    slot_tok = jnp.sum(jnp.where(chosen, adapter_slot[None, :], 0), axis=1)
    slot_hot = slot_tok[:, None] == jnp.arange(adapters, dtype=jnp.int32)[None, :]
    counts = lax.psum(jnp.sum(slot_hot.astype(jnp.float32), axis=0), "dp")
    first = lax.axis_index("dp") * per
    own_counts = lax.dynamic_slice(counts, (first,), (per,))
    mask = slot_tok[:, None] == jnp.arange(wide, dtype=jnp.int32)[None, :] // rank

    def squeeze(full):
        full = jnp.where(mask, full, 0.0)
        return sum(full[:, i : i + fold] for i in range(0, wide, fold))

    def spread(rows):
        return jnp.where(mask, jnp.tile(rows, (1, wide // fold)), 0).astype(jnp.bfloat16)

    up_all = lax.all_gather(up.reshape(per * rank, cols), "dp", axis=0, tiled=True)
    down_all = lax.all_gather(
        down.transpose(1, 0, 2).reshape(feat, per * rank), "dp", axis=1, tiled=True
    )
    weight_all = lax.all_gather(weight, "dp", axis=1, tiled=True)
    dy_all = lax.all_gather(dy, TP, axis=1, tiled=True)

    grad_low = squeeze(dot(dy, up_all, ((1,), (1,)))).astype(jnp.bfloat16)
    grad_low = lax.psum(grad_low, TP).astype(jnp.float32) * adapter_scale
    grad_low = spread(grad_low.astype(jnp.bfloat16))
    part_down = dot(grad_low, acts, ((0,), (0,))).astype(jnp.bfloat16)
    sum_down = lax.psum_scatter(part_down, "dp", scatter_dimension=0, tiled=True)

    low = squeeze(dot(acts, down_all, ((1,), (0,)))).astype(jnp.bfloat16)
    low = spread(lax.psum(low, TP))
    part_up = dot(low, dy, ((0,), (0,))).astype(jnp.bfloat16)
    sum_up = lax.psum_scatter(part_up, "dp", scatter_dimension=0, tiled=True)
    delta = adapter_scale * dot(low, up_all, ((1,), (0,)))

    base = dot(acts, weight_all, ((1,), (0,))).astype(jnp.bfloat16)
    base = lax.psum_scatter(base, TP, scatter_dimension=1, tiled=True)
    layer_out = (base.astype(jnp.float32) + delta).astype(jnp.bfloat16)
    input_gradient = (
        dot(dy_all, weight_all, ((1,), (1,))) + dot(grad_low, down_all, ((1,), (1,)))
    ).astype(jnp.bfloat16)
    grad_down = sum_down.astype(jnp.float32).reshape(per, rank, feat).transpose(0, 2, 1)
    grad_down = grad_down * (1.0 / own_counts)[:, None, None]
    grad_up = sum_up.astype(jnp.float32).reshape(per, rank, cols)
    grad_up = grad_up * (adapter_scale / own_counts)[:, None, None]
    return (layer_out, input_gradient, grad_down, grad_up)


LANES = 128
ROWS = 256


def fused_kernel(
    sizes,
    x_hbm, a_hbm, w_hbm, b_hbm, dy_hbm, slot_col, slot_row, cnt_ref,
    out_ref, ig_ref, down_ref, up_ref, cnt_out,
    x, a_all, w_all, b_all, dy_all, part, recv_r, recv_l, base_send, base_recv, acc,
    fold, grad_low, low, grad_t, lhs, gpack_send, gpack_recv, lpack_send, lpack_recv,
    up_send, up_recv, cnt_recv,
    load_sem, b_ss, b_rs, c_ss, c_rs, az_ss, az_rs, ay_ss, ay_rs, wz_ss, wz_rs, wy_ss, wy_rs,
    dy_ss, dy_rs, g_ss, g_rs, l_ss, l_rs, rs_ss, rr_rs, rl_rs, base_ss, base_rs, up_ss, up_rs,
):
    depth, pipes, peers, per, rank = sizes
    tok, feat = x.shape
    wide = per * rank
    pieces = wide // LANES
    each = LANES // rank
    i = lax.axis_index("dp")
    g = lax.axis_index("groups")
    k = lax.axis_index("tensor") * pipes + lax.axis_index("pipe")
    half = feat // 2
    mine = pl.ds(pl.multiple_of(g * half, half), half)
    other = pl.ds(pl.multiple_of((1 - g) * half, half), half)
    y_dev = {"groups": 1 - g}

    def tp_dev(kk):
        return {"tensor": kk // pipes, "pipe": kk % pipes}

    def rc(src, dst, ss, rs, dev):
        return pltpu.make_async_remote_copy(
            src_ref=src, dst_ref=dst, send_sem=ss, recv_sem=rs,
            device_id=dev, device_id_type=pl.DeviceIdType.MESH,
        )

    loads = [
        pltpu.make_async_copy(b_hbm, b_all.at[i], load_sem.at[0]),
        pltpu.make_async_copy(a_hbm, a_all.at[i], load_sem.at[1]),
        pltpu.make_async_copy(x_hbm, x, load_sem.at[2]),
        pltpu.make_async_copy(w_hbm, w_all.at[i], load_sem.at[3]),
        pltpu.make_async_copy(dy_hbm, dy_all.at[k], load_sem.at[4]),
    ]
    for c in loads:
        c.start()

    barrier = pltpu.get_barrier_semaphore()
    for q in range(1, depth):
        pl.semaphore_signal(barrier, inc=1, device_id={"dp": (i + q) % depth},
                            device_id_type=pl.DeviceIdType.MESH)
    for q in range(1, peers):
        pl.semaphore_signal(barrier, inc=1, device_id=tp_dev((k + q) % peers),
                            device_id_type=pl.DeviceIdType.MESH)
    pl.semaphore_signal(barrier, inc=1, device_id=y_dev, device_id_type=pl.DeviceIdType.MESH)
    pl.semaphore_wait(barrier, depth + peers - 1)

    def b_copy(j, src):
        return rc(b_all.at[src], b_all.at[src], b_ss.at[j], b_rs.at[src], {"dp": j})

    def c_copy(j, src):
        return rc(cnt_ref.at[j], cnt_recv.at[src], c_ss.at[j], c_rs.at[src], {"dp": j})

    def tp_copy(send, recv, ss, rs, kk, src):
        return rc(send, recv.at[src], ss.at[kk], rs.at[src], tp_dev(kk))

    def dy_copy(kk, src):
        return rc(dy_all.at[src], dy_all.at[src], dy_ss.at[kk], dy_rs.at[src], tp_dev(kk))

    def z_copy(buf, ss, rs, src, way, to):
        ref = buf.at[src, mine]
        return rc(ref, ref, ss.at[way, src], rs.at[src], {"dp": to})

    def y_copy(buf, ss, rs, src, rows):
        ref = buf.at[src, rows]
        return rc(ref, ref, ss.at[src], rs.at[src], y_dev)

    def own_sends(buf, ss, rs):
        @pl.when(i > 0)
        def _():
            z_copy(buf, ss, rs, i, 1, i - 1).start()

        @pl.when(i < depth - 1)
        def _():
            z_copy(buf, ss, rs, i, 0, i + 1).start()

    def ways(s, body):
        def step(way, carry):
            src = i + (2 * way - 1) * s

            @pl.when((src >= 0) & (src < depth))
            def _():
                body(src, way)

            return carry

        lax.fori_loop(0, 2, step, 0)

    def forward(buf, zs, zr, ys, yr, s):
        def body(src, way):
            to = i + 1 - 2 * way
            z_copy(buf, zs, zr, src, way, (i + 1) % depth).wait_recv()

            @pl.when((to >= 0) & (to < depth))
            def _():
                z_copy(buf, zs, zr, src, way, to).start()

            y_copy(buf, ys, yr, src, mine).start()

        ways(s, body)

    def drain(buf, zs, zr, ys, yr):
        @pl.when(i > 0)
        def _():
            z_copy(buf, zs, zr, i, 1, i - 1).wait_send()

        @pl.when(i < depth - 1)
        def _():
            z_copy(buf, zs, zr, i, 0, i + 1).wait_send()

        for s in range(1, depth):

            def body(src, way):
                to = i + 1 - 2 * way

                @pl.when((to >= 0) & (to < depth))
                def _():
                    z_copy(buf, zs, zr, src, way, to).wait_send()

                y_copy(buf, ys, yr, src, mine).wait_send()

            ways(s, body)

    lane_slot = lax.broadcasted_iota(jnp.int32, (ROWS, LANES), 1) // rank
    low_lanes = lax.broadcasted_iota(jnp.int32, (tok // 2, LANES), 1) < LANES // 2

    def tiles(n, body):
        def step(t, carry):
            body(t)
            return carry

        lax.fori_loop(0, n, step, 0)

    def rows_at(t, size=ROWS):
        return pl.ds(pl.multiple_of(t * size, size), size)

    def folded(z, j, rows):
        total = None
        for p in range(pieces):
            hit = slot_col[rows, :] == lane_slot + (per * j + each * p)
            term = jnp.where(hit, z[:, p * LANES : (p + 1) * LANES], 0.0)
            total = term if total is None else total + term
        return total

    def spread(values, j, rows):
        v = values[rows, :]
        out = [
            jnp.where(slot_col[rows, :] == lane_slot + (per * j + each * p), v, 0.0)
            for p in range(pieces)
        ]
        return jnp.concatenate(out, axis=1).astype(jnp.bfloat16)

    def transposed(values_t, j):
        for p in range(pieces):
            row_slot = lax.broadcasted_iota(jnp.int32, (LANES, tok), 0) // rank
            hit = slot_row[0:1, :] == row_slot + (per * j + each * p)
            lhs[p * LANES : (p + 1) * LANES, :] = jnp.where(hit, values_t[...], 0.0).astype(
                jnp.bfloat16
            )

    def pack(dst):
        f = fold[...]
        f = f + pltpu.roll(f, LANES // 2, 1)
        dst[...] = jnp.where(low_lanes, f[: tok // 2], f[tok // 2 :]).astype(jnp.bfloat16)

    def unpack(send, recv, ss, rs, dst, scale):
        total = send[...].astype(jnp.float32)
        for q in range(1, peers):
            kk = (k + q) % peers
            tp_copy(send, recv, ss, rs, kk, kk).wait_recv()
            total = total + recv[kk].astype(jnp.float32)
        total = (scale * total).astype(jnp.bfloat16).astype(jnp.float32)
        turned = pltpu.roll(total, LANES // 2, 1)
        dst[: tok // 2, :] = jnp.where(low_lanes, total, turned)
        dst[tok // 2 :, :] = jnp.where(low_lanes, turned, total)

    def low_add(j):
        def body(t):
            rows = rows_at(t)
            z = dot(x[rows, :], a_all[j], ((1,), (0,)))
            fold[rows, :] = fold[rows, :] + folded(z, j, rows)

        tiles(tok // ROWS, body)

    def base_block(j):
        def body(t):
            rows = rows_at(t)
            base_send[j, rows, :] = dot(x[rows, :], w_all[j], ((1,), (0,))).astype(jnp.bfloat16)

        tiles(tok // ROWS, body)

        @pl.when(j != k)
        def _():
            base_copy(j, k).start()

    def base_copy(j, src):
        return rc(base_send.at[j], base_recv.at[src], base_ss.at[j], base_rs.at[src], tp_dev(j))

    wide_cols = 512

    def back_a(j, first):
        def body(t):
            rows = rows_at(t)
            left = spread(grad_low, j, rows)

            def inner(c):
                cols = rows_at(c, wide_cols)
                z = dot(left, a_all[j, cols, :], ((1,), (1,)))
                acc[rows, cols] = z if first else acc[rows, cols] + z

            tiles(feat // wide_cols, inner)

        tiles(tok // ROWS, body)

    def back_w(j):
        def body(t):
            rows = rows_at(t)

            def inner(c):
                cols = rows_at(c, wide_cols)
                z = dot(dy_all[j, rows, :], w_all[j, cols, :], ((1,), (1,)))
                acc[rows, cols] = acc[rows, cols] + z

            tiles(feat // wide_cols, inner)

        tiles(tok // ROWS, body)

    def make_part(d):
        transposed(grad_t, d)

        def body(c):
            cols = rows_at(c, wide_cols)
            part[d, :, cols] = dot(lhs[...], x[:, cols], ((1,), (0,))).astype(jnp.bfloat16)

        tiles(feat // wide_cols, body)

    def add_to_part(d, recv):
        def body(c):
            cols = rows_at(c, wide_cols)
            total = part[d, :, cols].astype(jnp.float32) + recv[d, :, cols].astype(jnp.float32)
            part[d, :, cols] = total.astype(jnp.bfloat16)

        tiles(feat // wide_cols, body)

    def rs_up(d, to):
        return rc(part.at[d], recv_r.at[d], rs_ss.at[d], rr_rs.at[d], {"dp": to})

    def rs_down(d, to):
        return rc(part.at[d], recv_l.at[d], rs_ss.at[d], rl_rs.at[d], {"dp": to})

    def reduce_step(t):
        @pl.when(t >= i)
        def _():
            d = depth - 1 - t + i
            make_part(d)

            @pl.when(i > 0)
            def _():
                rs_up(d, i + 1).wait_recv()
                add_to_part(d, recv_r)

            rs_up(d, i + 1).start()

        @pl.when(t >= depth - 1 - i)
        def _():
            d = i - (depth - 1 - t)
            make_part(d)

            @pl.when(i < depth - 1)
            def _():
                rs_down(d, i - 1).wait_recv()
                add_to_part(d, recv_l)

            rs_down(d, i - 1).start()

    loads[0].wait()
    for q in range(1, depth):
        b_copy((i + q) % depth, i).start()
    for q in range(1, depth):
        c_copy((i + q) % depth, i).start()
    loads[1].wait()
    own_sends(a_all, az_ss, az_rs)
    loads[2].wait()
    loads[3].wait()
    base_block(i)

    loads[4].wait()
    fold[...] = jnp.zeros_like(fold)

    def grad_low_add(j):
        def body(t):
            rows = rows_at(t)
            z = dot(dy_all[k, rows, :], b_all[j], ((1,), (1,)))
            fold[rows, :] = fold[rows, :] + folded(z, j, rows)

        tiles(tok // ROWS, body)

    grad_low_add(i)

    def b_step(q, carry):
        j = (i + q) % depth
        b_copy(j, j).wait_recv()
        grad_low_add(j)
        return carry

    lax.fori_loop(1, depth, b_step, 0)
    pack(gpack_send)
    for q in range(1, peers):
        tp_copy(gpack_send, gpack_recv, g_ss, g_rs, (k + q) % peers, k).start()
    for q in range(1, peers):
        dy_copy((k + q) % peers, k).start()
    fold[...] = jnp.zeros_like(fold)
    low_add(i)
    unpack(gpack_send, gpack_recv, g_ss, g_rs, grad_low, adapter_scale)
    grad_t[...] = jnp.transpose(grad_low[...])

    def use_a(src, way):
        y_copy(a_all, ay_ss, ay_rs, src, other).wait_recv()
        low_add(src)
        back_a(src, False)

    for t in range(depth - 1):
        reduce_step(t)
        forward(a_all, az_ss, az_rs, ay_ss, ay_rs, t + 1)
        if t == 0:
            own_sends(w_all, wz_ss, wz_rs)
            back_a(i, True)
        else:
            ways(t, use_a)
    forward(w_all, wz_ss, wz_rs, wy_ss, wy_rs, 1)
    ways(depth - 1, use_a)
    pack(lpack_send)
    for q in range(1, peers):
        tp_copy(lpack_send, lpack_recv, l_ss, l_rs, (k + q) % peers, k).start()
    for q in range(1, peers):
        kk = (k + q) % peers
        dy_copy(kk, kk).wait_recv()
    back_w(i)
    unpack(lpack_send, lpack_recv, l_ss, l_rs, low, 1.0)
    grad_t[...] = jnp.transpose(low[...])

    def up_copy(j, src):
        return rc(up_send.at[j], up_recv.at[src], up_ss.at[j], up_rs.at[src], {"dp": j})

    def up_part(q, carry):
        j = (i + q) % depth
        transposed(grad_t, j)
        up_send[j] = dot(lhs[...], dy_all[k], ((1,), (0,))).astype(jnp.bfloat16)

        @pl.when(q < depth)
        def _():
            up_copy(j, i).start()

        return carry

    lax.fori_loop(1, depth + 1, up_part, 0)

    def use_w(src, way):
        y_copy(w_all, wy_ss, wy_rs, src, other).wait_recv()
        base_block(src)
        back_w(src)

    for s in range(2, depth):
        forward(w_all, wz_ss, wz_rs, wy_ss, wy_rs, s)
        ways(s - 1, use_w)

    grad_t[...] = jnp.transpose(grad_low[...])
    make_part(i)

    @pl.when(i > 0)
    def _():
        rs_up(i, (i + 1) % depth).wait_recv()
        add_to_part(i, recv_r)

    @pl.when(i < depth - 1)
    def _():
        rs_down(i, (i + 1) % depth).wait_recv()
        add_to_part(i, recv_l)

    def down_out(c):
        cols = rows_at(c, wide_cols)
        down_ref[:, cols] = part[i, :, cols].astype(jnp.float32)

    tiles(feat // wide_cols, down_out)

    ways(depth - 1, use_w)

    total = up_send[i].astype(jnp.float32)
    cnt = cnt_ref[i]
    for q in range(1, depth):
        j = (i + q) % depth
        up_copy(j, j).wait_recv()
        total = total + up_recv[j].astype(jnp.float32)
        c_copy(j, j).wait_recv()
        cnt = cnt + cnt_recv[j]
    up_ref[...] = total
    cnt_out[...] = cnt

    def ig_out(t):
        rows = rows_at(t, 64)
        ig_ref[rows, :] = acc[rows, :].astype(jnp.bfloat16)

    tiles(tok // 64, ig_out)

    for q in range(1, peers):
        kk = (k + q) % peers
        base_copy(kk, kk).wait_recv()

    def finish(t):
        rows = rows_at(t)
        delta = None
        for j in range(depth):
            z = dot(spread(low, j, rows), b_all[j], ((1,), (0,)))
            delta = z if delta is None else delta + z
        delta = (adapter_scale * delta).astype(jnp.bfloat16).astype(jnp.float32)
        base = base_send[k, rows, :].astype(jnp.float32)
        for q in range(1, peers):
            base = base + base_recv[(k + q) % peers, rows, :].astype(jnp.float32)
        out_ref[rows, :] = (base + delta).astype(jnp.bfloat16)

    tiles(tok // ROWS, finish)

    drain(a_all, az_ss, az_rs, ay_ss, ay_rs)
    drain(w_all, wz_ss, wz_rs, wy_ss, wy_rs)
    for q in range(1, depth):
        j = (i + q) % depth
        b_copy(j, i).wait_send()
        c_copy(j, i).wait_send()
        up_copy(j, i).wait_send()
        rs_up(j, j).wait_send()
    for q in range(1, peers):
        kk = (k + q) % peers
        tp_copy(gpack_send, gpack_recv, g_ss, g_rs, kk, k).wait_send()
        tp_copy(lpack_send, lpack_recv, l_ss, l_rs, kk, k).wait_send()
        dy_copy(kk, k).wait_send()
        base_copy(kk, k).wait_send()


def fused(mesh_sizes, acts, weight, down, up, dy, token_adapter, adapter_slot):
    depth, pipes, peers = mesh_sizes
    per, feat, rank = down.shape
    cols = up.shape[2]
    tok = acts.shape[0]
    adapters = adapter_slot.shape[0]
    wide = per * rank
    ids = token_adapter[:, 0]
    everyone = jnp.arange(adapters, dtype=jnp.int32)
    slot_tok = jnp.sum(jnp.where(ids[:, None] == everyone[None, :], adapter_slot[None, :], 0), axis=1)
    counts = jnp.sum((slot_tok[:, None] == everyone[None, :]).astype(jnp.float32), axis=0)
    cnt = jnp.broadcast_to(jnp.repeat(counts, rank).reshape(depth, 1, wide), (depth, 8, wide))
    slot_col = jnp.broadcast_to(slot_tok[:, None], (tok, LANES))
    slot_row = jnp.broadcast_to(slot_tok[None, :], (8, tok))
    a = down.transpose(1, 0, 2).reshape(feat, wide)
    b = up.reshape(wide, cols)
    bf, f32 = jnp.bfloat16, jnp.float32
    dma = pltpu.SemaphoreType.DMA
    vmem = pl.BlockSpec(memory_space=pltpu.VMEM)
    hbm = pl.BlockSpec(memory_space=pl.ANY)
    layer_out, ig, sum_down, sum_up, total = pl.pallas_call(
        functools.partial(fused_kernel, (depth, pipes, peers, per, rank)),
        out_shape=(
            jax.ShapeDtypeStruct((tok, cols), bf),
            jax.ShapeDtypeStruct((tok, feat), bf),
            jax.ShapeDtypeStruct((wide, feat), f32),
            jax.ShapeDtypeStruct((wide, cols), f32),
            jax.ShapeDtypeStruct((8, wide), f32),
        ),
        in_specs=[hbm] * 5 + [vmem] * 3,
        out_specs=(vmem,) * 5,
        scratch_shapes=[
            pltpu.VMEM((tok, feat), bf),
            pltpu.VMEM((depth, feat, wide), bf),
            pltpu.VMEM((depth, feat, cols), bf),
            pltpu.VMEM((depth, wide, cols), bf),
            pltpu.VMEM((peers, tok, cols), bf),
            pltpu.VMEM((depth, wide, feat), bf),
            pltpu.VMEM((depth, wide, feat), bf),
            pltpu.VMEM((depth, wide, feat), bf),
            pltpu.VMEM((peers, tok, cols), bf),
            pltpu.VMEM((peers, tok, cols), bf),
            pltpu.VMEM((tok, feat), f32),
            pltpu.VMEM((tok, LANES), f32),
            pltpu.VMEM((tok, LANES), f32),
            pltpu.VMEM((tok, LANES), f32),
            pltpu.VMEM((LANES, tok), f32),
            pltpu.VMEM((wide, tok), bf),
            pltpu.VMEM((tok // 2, LANES), bf),
            pltpu.VMEM((peers, tok // 2, LANES), bf),
            pltpu.VMEM((tok // 2, LANES), bf),
            pltpu.VMEM((peers, tok // 2, LANES), bf),
            pltpu.VMEM((depth, wide, cols), bf),
            pltpu.VMEM((depth, wide, cols), bf),
            pltpu.VMEM((depth, 8, wide), f32),
            dma((5,)),
            dma((depth,)), dma((depth,)), dma((depth,)), dma((depth,)),
            dma((2, depth)), dma((depth,)), dma((depth,)), dma((depth,)),
            dma((2, depth)), dma((depth,)), dma((depth,)), dma((depth,)),
            dma((peers,)), dma((peers,)), dma((peers,)), dma((peers,)),
            dma((peers,)), dma((peers,)),
            dma((depth,)), dma((depth,)), dma((depth,)),
            dma((peers,)), dma((peers,)), dma((depth,)), dma((depth,)),
        ],
        compiler_params=pltpu.CompilerParams(
            collective_id=0, has_side_effects=True, vmem_limit_bytes=60 * 1024 * 1024
        ),
    )(acts, a, weight, b, dy, slot_col, slot_row, cnt)
    own = total[0].reshape(per, rank)[:, 0]
    grad_down = sum_down.reshape(per, rank, feat).transpose(0, 2, 1)
    grad_down = grad_down * (1.0 / own)[:, None, None]
    grad_up = sum_up.reshape(per, rank, cols) * (adapter_scale / own)[:, None, None]
    return (layer_out, ig, grad_down, grad_up)


def local(mesh_sizes, groups, *args):
    acts, weight, down, up, dy, _, adapter_slot = args
    depth, pipes, peers = mesh_sizes
    per, feat, rank = down.shape
    tok, cols = dy.shape
    fits = (
        groups == 2 and depth == peers and LANES == 2 * rank and per * rank % LANES == 0
        and cols % LANES == 0 and weight.shape[1] == cols and tok % 512 == 0
        and feat % 1024 == 0 and per * rank <= 256 and cols <= 256 and tok * feat <= 1 << 21
        and depth <= 4
    )
    if fits:
        return fused(mesh_sizes, *args)
    return plain(*args)


def solution(mesh):
    shape = mesh.shape
    sizes = (shape["dp"], shape["pipe"], shape["tensor"] * shape["pipe"])
    return jax.shard_map(
        functools.partial(local, sizes, shape["groups"]),
        mesh=mesh,
        in_specs=(
            P(("groups", "dp"), TP),
            P(TP, "dp"),
            P("dp", TP, None),
            P("dp", None, TP),
            P(("groups", "dp"), TP),
            P(("groups", "dp"), None),
            P(),
        ),
        out_specs=(
            P(("groups", "dp"), TP),
            P(("groups", "dp"), TP),
            P(("groups", "dp"), TP, None),
            P(("groups", "dp"), None, TP),
        ),
        check_vma=False,
    )
```

```python
import functools

import jax
import jax.numpy as jnp
from jax import lax
from jax.experimental import pallas as pl
from jax.experimental.pallas import tpu as pltpu
from jax.sharding import PartitionSpec as P

adapter_scale = 2.0
TP = ("tensor", "pipe")


def dot(a, b, dims):
    return lax.dot_general(a, b, (dims, ((), ())), preferred_element_type=jnp.float32)


def plain(acts, weight, down, up, dy, token_adapter, adapter_slot):
    per, feat, rank = down.shape
    cols = up.shape[2]
    tok = acts.shape[0]
    adapters = adapter_slot.shape[0]
    wide = adapters * rank
    fold = 2 * rank
    ids = token_adapter[:, 0]
    chosen = ids[:, None] == jnp.arange(adapters, dtype=jnp.int32)[None, :]
    slot_tok = jnp.sum(jnp.where(chosen, adapter_slot[None, :], 0), axis=1)
    slot_hot = slot_tok[:, None] == jnp.arange(adapters, dtype=jnp.int32)[None, :]
    counts = lax.psum(jnp.sum(slot_hot.astype(jnp.float32), axis=0), "dp")
    first = lax.axis_index("dp") * per
    own_counts = lax.dynamic_slice(counts, (first,), (per,))
    mask = slot_tok[:, None] == jnp.arange(wide, dtype=jnp.int32)[None, :] // rank

    def squeeze(full):
        full = jnp.where(mask, full, 0.0)
        return sum(full[:, i : i + fold] for i in range(0, wide, fold))

    def spread(rows):
        return jnp.where(mask, jnp.tile(rows, (1, wide // fold)), 0).astype(jnp.bfloat16)

    up_all = lax.all_gather(up.reshape(per * rank, cols), "dp", axis=0, tiled=True)
    down_all = lax.all_gather(
        down.transpose(1, 0, 2).reshape(feat, per * rank), "dp", axis=1, tiled=True
    )
    weight_all = lax.all_gather(weight, "dp", axis=1, tiled=True)
    dy_all = lax.all_gather(dy, TP, axis=1, tiled=True)

    grad_low = squeeze(dot(dy, up_all, ((1,), (1,)))).astype(jnp.bfloat16)
    grad_low = lax.psum(grad_low, TP).astype(jnp.float32) * adapter_scale
    grad_low = spread(grad_low.astype(jnp.bfloat16))
    part_down = dot(grad_low, acts, ((0,), (0,))).astype(jnp.bfloat16)
    sum_down = lax.psum_scatter(part_down, "dp", scatter_dimension=0, tiled=True)

    low = squeeze(dot(acts, down_all, ((1,), (0,)))).astype(jnp.bfloat16)
    low = spread(lax.psum(low, TP))
    part_up = dot(low, dy, ((0,), (0,))).astype(jnp.bfloat16)
    sum_up = lax.psum_scatter(part_up, "dp", scatter_dimension=0, tiled=True)
    delta = adapter_scale * dot(low, up_all, ((1,), (0,)))

    base = dot(acts, weight_all, ((1,), (0,))).astype(jnp.bfloat16)
    base = lax.psum_scatter(base, TP, scatter_dimension=1, tiled=True)
    layer_out = (base.astype(jnp.float32) + delta).astype(jnp.bfloat16)
    input_gradient = (
        dot(dy_all, weight_all, ((1,), (1,))) + dot(grad_low, down_all, ((1,), (1,)))
    ).astype(jnp.bfloat16)
    grad_down = sum_down.astype(jnp.float32).reshape(per, rank, feat).transpose(0, 2, 1)
    grad_down = grad_down * (1.0 / own_counts)[:, None, None]
    grad_up = sum_up.astype(jnp.float32).reshape(per, rank, cols)
    grad_up = grad_up * (adapter_scale / own_counts)[:, None, None]
    return (layer_out, input_gradient, grad_down, grad_up)


LANES = 128
ROWS = 256


def fused_kernel(
    sizes,
    x_hbm, a_hbm, w_hbm, b_hbm, dy_hbm, slot_col, slot_row, cnt_ref,
    out_ref, ig_ref, down_ref, up_ref, cnt_out,
    x, a_all, w_all, b_all, dy_all, part, recv_r, recv_l, base_send, base_recv, acc,
    fold, grad_low, low, grad_t, lhs, gpack_send, gpack_recv, lpack_send, lpack_recv,
    up_send, up_recv, cnt_recv,
    load_sem, b_ss, b_rs, c_ss, c_rs, az_ss, az_rs, ay_ss, ay_rs, wz_ss, wz_rs, wy_ss, wy_rs,
    dy_ss, dy_rs, g_ss, g_rs, l_ss, l_rs, rs_ss, rr_rs, rl_rs, base_ss, base_rs, up_ss, up_rs,
):
    depth, pipes, peers, per, rank = sizes
    tok, feat = x.shape
    wide = per * rank
    pieces = wide // LANES
    each = LANES // rank
    i = lax.axis_index("dp")
    g = lax.axis_index("groups")
    k = lax.axis_index("tensor") * pipes + lax.axis_index("pipe")
    half = feat // 2
    mine = pl.ds(pl.multiple_of(g * half, half), half)
    other = pl.ds(pl.multiple_of((1 - g) * half, half), half)
    y_dev = {"groups": 1 - g}

    def tp_dev(kk):
        return {"tensor": kk // pipes, "pipe": kk % pipes}

    def rc(src, dst, ss, rs, dev):
        return pltpu.make_async_remote_copy(
            src_ref=src, dst_ref=dst, send_sem=ss, recv_sem=rs,
            device_id=dev, device_id_type=pl.DeviceIdType.MESH,
        )

    loads = [
        pltpu.make_async_copy(b_hbm, b_all.at[i], load_sem.at[0]),
        pltpu.make_async_copy(a_hbm, a_all.at[i], load_sem.at[1]),
        pltpu.make_async_copy(x_hbm, x, load_sem.at[2]),
        pltpu.make_async_copy(w_hbm, w_all.at[i], load_sem.at[3]),
        pltpu.make_async_copy(dy_hbm, dy_all.at[k], load_sem.at[4]),
    ]
    for c in loads:
        c.start()

    barrier = pltpu.get_barrier_semaphore()
    for q in range(1, depth):
        pl.semaphore_signal(barrier, inc=1, device_id={"dp": (i + q) % depth},
                            device_id_type=pl.DeviceIdType.MESH)
    for q in range(1, peers):
        pl.semaphore_signal(barrier, inc=1, device_id=tp_dev((k + q) % peers),
                            device_id_type=pl.DeviceIdType.MESH)
    pl.semaphore_signal(barrier, inc=1, device_id=y_dev, device_id_type=pl.DeviceIdType.MESH)
    pl.semaphore_wait(barrier, depth + peers - 1)

    def b_copy(j, src):
        return rc(b_all.at[src], b_all.at[src], b_ss.at[j], b_rs.at[src], {"dp": j})

    def c_copy(j, src):
        return rc(cnt_ref.at[j], cnt_recv.at[src], c_ss.at[j], c_rs.at[src], {"dp": j})

    def tp_copy(send, recv, ss, rs, kk, src):
        return rc(send, recv.at[src], ss.at[kk], rs.at[src], tp_dev(kk))

    def dy_copy(kk, src):
        return rc(dy_all.at[src], dy_all.at[src], dy_ss.at[kk], dy_rs.at[src], tp_dev(kk))

    def z_copy(buf, ss, rs, src, way, to):
        ref = buf.at[src, mine]
        return rc(ref, ref, ss.at[way, src], rs.at[src], {"dp": to})

    def y_copy(buf, ss, rs, src, rows):
        ref = buf.at[src, rows]
        return rc(ref, ref, ss.at[src], rs.at[src], y_dev)

    def own_sends(buf, ss, rs):
        @pl.when(i > 0)
        def _():
            z_copy(buf, ss, rs, i, 1, i - 1).start()

        @pl.when(i < depth - 1)
        def _():
            z_copy(buf, ss, rs, i, 0, i + 1).start()

    def ways(s, body):
        def step(way, carry):
            src = i + (2 * way - 1) * s

            @pl.when((src >= 0) & (src < depth))
            def _():
                body(src, way)

            return carry

        lax.fori_loop(0, 2, step, 0)

    def forward(buf, zs, zr, ys, yr, s):
        def body(src, way):
            to = i + 1 - 2 * way
            z_copy(buf, zs, zr, src, way, (i + 1) % depth).wait_recv()

            @pl.when((to >= 0) & (to < depth))
            def _():
                z_copy(buf, zs, zr, src, way, to).start()

            y_copy(buf, ys, yr, src, mine).start()

        ways(s, body)

    def drain(buf, zs, zr, ys, yr):
        @pl.when(i > 0)
        def _():
            z_copy(buf, zs, zr, i, 1, i - 1).wait_send()

        @pl.when(i < depth - 1)
        def _():
            z_copy(buf, zs, zr, i, 0, i + 1).wait_send()

        for s in range(1, depth):

            def body(src, way):
                to = i + 1 - 2 * way

                @pl.when((to >= 0) & (to < depth))
                def _():
                    z_copy(buf, zs, zr, src, way, to).wait_send()

                y_copy(buf, ys, yr, src, mine).wait_send()

            ways(s, body)

    lane_slot = lax.broadcasted_iota(jnp.int32, (ROWS, LANES), 1) // rank
    low_lanes = lax.broadcasted_iota(jnp.int32, (tok // 2, LANES), 1) < LANES // 2

    def tiles(n, body):
        def step(t, carry):
            body(t)
            return carry

        lax.fori_loop(0, n, step, 0)

    def rows_at(t, size=ROWS):
        return pl.ds(pl.multiple_of(t * size, size), size)

    def folded(z, j, rows):
        total = None
        for p in range(pieces):
            hit = slot_col[rows, :] == lane_slot + (per * j + each * p)
            term = jnp.where(hit, z[:, p * LANES : (p + 1) * LANES], 0.0)
            total = term if total is None else total + term
        return total

    def spread(values, j, rows):
        v = values[rows, :]
        out = [
            jnp.where(slot_col[rows, :] == lane_slot + (per * j + each * p), v, 0.0)
            for p in range(pieces)
        ]
        return jnp.concatenate(out, axis=1).astype(jnp.bfloat16)

    def transposed(values_t, j):
        for p in range(pieces):
            row_slot = lax.broadcasted_iota(jnp.int32, (LANES, tok), 0) // rank
            hit = slot_row[0:1, :] == row_slot + (per * j + each * p)
            lhs[p * LANES : (p + 1) * LANES, :] = jnp.where(hit, values_t[...], 0.0).astype(
                jnp.bfloat16
            )

    def pack(dst):
        f = fold[...]
        f = f + pltpu.roll(f, LANES // 2, 1)
        dst[...] = jnp.where(low_lanes, f[: tok // 2], f[tok // 2 :]).astype(jnp.bfloat16)

    def unpack(send, recv, ss, rs, dst, scale):
        total = send[...].astype(jnp.float32)
        for q in range(1, peers):
            kk = (k + q) % peers
            tp_copy(send, recv, ss, rs, kk, kk).wait_recv()
            total = total + recv[kk].astype(jnp.float32)
        total = (scale * total).astype(jnp.bfloat16).astype(jnp.float32)
        turned = pltpu.roll(total, LANES // 2, 1)
        dst[: tok // 2, :] = jnp.where(low_lanes, total, turned)
        dst[tok // 2 :, :] = jnp.where(low_lanes, turned, total)

    def low_add(j):
        def body(t):
            rows = rows_at(t)
            z = dot(x[rows, :], a_all[j], ((1,), (0,)))
            fold[rows, :] = fold[rows, :] + folded(z, j, rows)

        tiles(tok // ROWS, body)

    def base_block(j):
        def body(t):
            rows = rows_at(t)
            base_send[j, rows, :] = dot(x[rows, :], w_all[j], ((1,), (0,))).astype(jnp.bfloat16)

        tiles(tok // ROWS, body)

        @pl.when(j != k)
        def _():
            base_copy(j, k).start()

    def base_copy(j, src):
        return rc(base_send.at[j], base_recv.at[src], base_ss.at[j], base_rs.at[src], tp_dev(j))

    wide_cols = 512

    def back_a(j, first):
        def body(t):
            rows = rows_at(t)
            left = spread(grad_low, j, rows)

            def inner(c):
                cols = rows_at(c, wide_cols)
                z = dot(left, a_all[j, cols, :], ((1,), (1,)))
                acc[rows, cols] = z if first else acc[rows, cols] + z

            tiles(feat // wide_cols, inner)

        tiles(tok // ROWS, body)

    def back_w(j):
        def body(t):
            rows = rows_at(t)

            def inner(c):
                cols = rows_at(c, wide_cols)
                z = dot(dy_all[j, rows, :], w_all[j, cols, :], ((1,), (1,)))
                acc[rows, cols] = acc[rows, cols] + z

            tiles(feat // wide_cols, inner)

        tiles(tok // ROWS, body)

    def make_part(d, h):
        transposed(grad_t, d)

        def body(c):
            cols = rows_at(c + h * half_tiles, wide_cols)
            part[d, :, cols] = dot(lhs[...], x[:, cols], ((1,), (0,))).astype(jnp.bfloat16)

        tiles(half_tiles, body)

    half_tiles = half // wide_cols

    def add_to_part(d, h, recv):
        def body(c):
            cols = rows_at(c + h * half_tiles, wide_cols)
            total = part[d, :, cols].astype(jnp.float32) + recv[d, :, cols].astype(jnp.float32)
            part[d, :, cols] = total.astype(jnp.bfloat16)

        tiles(half_tiles, body)

    def rs_up(d, h, to):
        at = (d, slice(None), pl.ds(h * half, half))
        return rc(part.at[at], recv_r.at[at], rs_ss.at[h, d], rr_rs.at[h, d], {"dp": to})

    def rs_down(d, h, to):
        at = (d, slice(None), pl.ds(h * half, half))
        return rc(part.at[at], recv_l.at[at], rs_ss.at[h, d], rl_rs.at[h, d], {"dp": to})

    def reduce_step(t, h):
        @pl.when(t >= i)
        def _():
            d = depth - 1 - t + i
            make_part(d, h)

            @pl.when(i > 0)
            def _():
                rs_up(d, h, i + 1).wait_recv()
                add_to_part(d, h, recv_r)

            rs_up(d, h, i + 1).start()

        @pl.when(t >= depth - 1 - i)
        def _():
            d = i - (depth - 1 - t)
            make_part(d, h)

            @pl.when(i < depth - 1)
            def _():
                rs_down(d, h, i - 1).wait_recv()
                add_to_part(d, h, recv_l)

            rs_down(d, h, i - 1).start()

    loads[0].wait()
    for q in range(1, depth):
        b_copy((i + q) % depth, i).start()
    for q in range(1, depth):
        c_copy((i + q) % depth, i).start()
    loads[1].wait()
    own_sends(a_all, az_ss, az_rs)
    loads[2].wait()
    loads[3].wait()
    base_block(i)

    loads[4].wait()
    fold[...] = jnp.zeros_like(fold)

    def grad_low_add(j):
        def body(t):
            rows = rows_at(t)
            z = dot(dy_all[k, rows, :], b_all[j], ((1,), (1,)))
            fold[rows, :] = fold[rows, :] + folded(z, j, rows)

        tiles(tok // ROWS, body)

    grad_low_add(i)

    def b_step(q, carry):
        j = (i + q) % depth
        b_copy(j, j).wait_recv()
        grad_low_add(j)
        return carry

    lax.fori_loop(1, depth, b_step, 0)
    pack(gpack_send)
    for q in range(1, peers):
        tp_copy(gpack_send, gpack_recv, g_ss, g_rs, (k + q) % peers, k).start()
    for q in range(1, peers):
        dy_copy((k + q) % peers, k).start()
    fold[...] = jnp.zeros_like(fold)
    low_add(i)
    unpack(gpack_send, gpack_recv, g_ss, g_rs, grad_low, adapter_scale)
    grad_t[...] = jnp.transpose(grad_low[...])

    def use_a(src, way):
        y_copy(a_all, ay_ss, ay_rs, src, other).wait_recv()
        low_add(src)
        back_a(src, False)

    def forward_a(step):
        forward(a_all, az_ss, az_rs, ay_ss, ay_rs, step)

    def forward_w(step):
        forward(w_all, wz_ss, wz_rs, wy_ss, wy_rs, step)

    last = depth - 1
    reduce_step(0, 0)
    forward_a(1)
    reduce_step(0, 1)
    back_a(i, True)
    for t in range(1, last):
        forward_a(t + 1)
        if t == 1:
            own_sends(w_all, wz_ss, wz_rs)
        ways(t, use_a)
        reduce_step(t, 0)
        if t > 1:
            forward_w(t - 1)
        reduce_step(t, 1)
    if last == 1:
        own_sends(w_all, wz_ss, wz_rs)
    ways(last, use_a)
    pack(lpack_send)
    for q in range(1, peers):
        tp_copy(lpack_send, lpack_recv, l_ss, l_rs, (k + q) % peers, k).start()
    for q in range(1, peers):
        kk = (k + q) % peers
        dy_copy(kk, kk).wait_recv()
    sent = max(0, last - 2)
    if sent < last:
        forward_w(sent + 1)
    back_w(i)
    unpack(lpack_send, lpack_recv, l_ss, l_rs, low, 1.0)
    grad_t[...] = jnp.transpose(low[...])

    def up_copy(j, src):
        return rc(up_send.at[j], up_recv.at[src], up_ss.at[j], up_rs.at[src], {"dp": j})

    def up_part(q, carry):
        j = (i + q) % depth
        transposed(grad_t, j)
        up_send[j] = dot(lhs[...], dy_all[k], ((1,), (0,))).astype(jnp.bfloat16)

        @pl.when(q < depth)
        def _():
            up_copy(j, i).start()

        return carry

    lax.fori_loop(1, depth + 1, up_part, 0)

    def use_w(src, way):
        y_copy(w_all, wy_ss, wy_rs, src, other).wait_recv()
        base_block(src)
        back_w(src)

    for step in range(sent + 2, depth):
        forward_w(step)
        ways(step - 1, use_w)
    for step in range(1, min(sent + 1, last)):
        ways(step, use_w)

    grad_t[...] = jnp.transpose(grad_low[...])
    for h in range(2):
        make_part(i, h)

        @pl.when(i > 0)
        def _():
            rs_up(i, h, (i + 1) % depth).wait_recv()
            add_to_part(i, h, recv_r)

        @pl.when(i < depth - 1)
        def _():
            rs_down(i, h, (i + 1) % depth).wait_recv()
            add_to_part(i, h, recv_l)

    def down_out(c):
        cols = rows_at(c, wide_cols)
        down_ref[:, cols] = part[i, :, cols].astype(jnp.float32)

    tiles(feat // wide_cols, down_out)

    ways(depth - 1, use_w)

    total = up_send[i].astype(jnp.float32)
    cnt = cnt_ref[i]
    for q in range(1, depth):
        j = (i + q) % depth
        up_copy(j, j).wait_recv()
        total = total + up_recv[j].astype(jnp.float32)
        c_copy(j, j).wait_recv()
        cnt = cnt + cnt_recv[j]
    up_ref[...] = total
    cnt_out[...] = cnt

    def ig_out(t):
        rows = rows_at(t, 64)
        ig_ref[rows, :] = acc[rows, :].astype(jnp.bfloat16)

    tiles(tok // 64, ig_out)

    for q in range(1, peers):
        kk = (k + q) % peers
        base_copy(kk, kk).wait_recv()

    def finish(t):
        rows = rows_at(t)
        delta = None
        for j in range(depth):
            z = dot(spread(low, j, rows), b_all[j], ((1,), (0,)))
            delta = z if delta is None else delta + z
        delta = (adapter_scale * delta).astype(jnp.bfloat16).astype(jnp.float32)
        base = base_send[k, rows, :].astype(jnp.float32)
        for q in range(1, peers):
            base = base + base_recv[(k + q) % peers, rows, :].astype(jnp.float32)
        out_ref[rows, :] = (base + delta).astype(jnp.bfloat16)

    tiles(tok // ROWS, finish)

    drain(a_all, az_ss, az_rs, ay_ss, ay_rs)
    drain(w_all, wz_ss, wz_rs, wy_ss, wy_rs)
    for q in range(1, depth):
        j = (i + q) % depth
        b_copy(j, i).wait_send()
        c_copy(j, i).wait_send()
        up_copy(j, i).wait_send()
        rs_up(j, 0, j).wait_send()
        rs_up(j, 1, j).wait_send()
    for q in range(1, peers):
        kk = (k + q) % peers
        tp_copy(gpack_send, gpack_recv, g_ss, g_rs, kk, k).wait_send()
        tp_copy(lpack_send, lpack_recv, l_ss, l_rs, kk, k).wait_send()
        dy_copy(kk, k).wait_send()
        base_copy(kk, k).wait_send()


def fused(mesh_sizes, acts, weight, down, up, dy, token_adapter, adapter_slot):
    depth, pipes, peers = mesh_sizes
    per, feat, rank = down.shape
    cols = up.shape[2]
    tok = acts.shape[0]
    adapters = adapter_slot.shape[0]
    wide = per * rank
    ids = token_adapter[:, 0]
    everyone = jnp.arange(adapters, dtype=jnp.int32)
    slot_tok = jnp.sum(jnp.where(ids[:, None] == everyone[None, :], adapter_slot[None, :], 0), axis=1)
    counts = jnp.sum((slot_tok[:, None] == everyone[None, :]).astype(jnp.float32), axis=0)
    cnt = jnp.broadcast_to(jnp.repeat(counts, rank).reshape(depth, 1, wide), (depth, 8, wide))
    slot_col = jnp.broadcast_to(slot_tok[:, None], (tok, LANES))
    slot_row = jnp.broadcast_to(slot_tok[None, :], (8, tok))
    a = down.transpose(1, 0, 2).reshape(feat, wide)
    b = up.reshape(wide, cols)
    bf, f32 = jnp.bfloat16, jnp.float32
    dma = pltpu.SemaphoreType.DMA
    vmem = pl.BlockSpec(memory_space=pltpu.VMEM)
    hbm = pl.BlockSpec(memory_space=pl.ANY)
    layer_out, ig, sum_down, sum_up, total = pl.pallas_call(
        functools.partial(fused_kernel, (depth, pipes, peers, per, rank)),
        out_shape=(
            jax.ShapeDtypeStruct((tok, cols), bf),
            jax.ShapeDtypeStruct((tok, feat), bf),
            jax.ShapeDtypeStruct((wide, feat), f32),
            jax.ShapeDtypeStruct((wide, cols), f32),
            jax.ShapeDtypeStruct((8, wide), f32),
        ),
        in_specs=[hbm] * 5 + [vmem] * 3,
        out_specs=(vmem,) * 5,
        scratch_shapes=[
            pltpu.VMEM((tok, feat), bf),
            pltpu.VMEM((depth, feat, wide), bf),
            pltpu.VMEM((depth, feat, cols), bf),
            pltpu.VMEM((depth, wide, cols), bf),
            pltpu.VMEM((peers, tok, cols), bf),
            pltpu.VMEM((depth, wide, feat), bf),
            pltpu.VMEM((depth, wide, feat), bf),
            pltpu.VMEM((depth, wide, feat), bf),
            pltpu.VMEM((peers, tok, cols), bf),
            pltpu.VMEM((peers, tok, cols), bf),
            pltpu.VMEM((tok, feat), f32),
            pltpu.VMEM((tok, LANES), f32),
            pltpu.VMEM((tok, LANES), f32),
            pltpu.VMEM((tok, LANES), f32),
            pltpu.VMEM((LANES, tok), f32),
            pltpu.VMEM((wide, tok), bf),
            pltpu.VMEM((tok // 2, LANES), bf),
            pltpu.VMEM((peers, tok // 2, LANES), bf),
            pltpu.VMEM((tok // 2, LANES), bf),
            pltpu.VMEM((peers, tok // 2, LANES), bf),
            pltpu.VMEM((depth, wide, cols), bf),
            pltpu.VMEM((depth, wide, cols), bf),
            pltpu.VMEM((depth, 8, wide), f32),
            dma((5,)),
            dma((depth,)), dma((depth,)), dma((depth,)), dma((depth,)),
            dma((2, depth)), dma((depth,)), dma((depth,)), dma((depth,)),
            dma((2, depth)), dma((depth,)), dma((depth,)), dma((depth,)),
            dma((peers,)), dma((peers,)), dma((peers,)), dma((peers,)),
            dma((peers,)), dma((peers,)),
            dma((2, depth)), dma((2, depth)), dma((2, depth)),
            dma((peers,)), dma((peers,)), dma((depth,)), dma((depth,)),
        ],
        compiler_params=pltpu.CompilerParams(
            collective_id=0, has_side_effects=True, vmem_limit_bytes=60 * 1024 * 1024
        ),
    )(acts, a, weight, b, dy, slot_col, slot_row, cnt)
    own = total[0].reshape(per, rank)[:, 0]
    grad_down = sum_down.reshape(per, rank, feat).transpose(0, 2, 1)
    grad_down = grad_down * (1.0 / own)[:, None, None]
    grad_up = sum_up.reshape(per, rank, cols) * (adapter_scale / own)[:, None, None]
    return (layer_out, ig, grad_down, grad_up)


def local(mesh_sizes, groups, *args):
    acts, weight, down, up, dy, _, adapter_slot = args
    depth, pipes, peers = mesh_sizes
    per, feat, rank = down.shape
    tok, cols = dy.shape
    fits = (
        groups == 2 and depth == peers and LANES == 2 * rank and per * rank % LANES == 0
        and cols % LANES == 0 and weight.shape[1] == cols and tok % 512 == 0
        and feat % 1024 == 0 and per * rank <= 256 and cols <= 256 and tok * feat <= 1 << 21
        and depth <= 4
    )
    if fits:
        return fused(mesh_sizes, *args)
    return plain(*args)


def solution(mesh):
    shape = mesh.shape
    sizes = (shape["dp"], shape["pipe"], shape["tensor"] * shape["pipe"])
    return jax.shard_map(
        functools.partial(local, sizes, shape["groups"]),
        mesh=mesh,
        in_specs=(
            P(("groups", "dp"), TP),
            P(TP, "dp"),
            P("dp", TP, None),
            P("dp", None, TP),
            P(("groups", "dp"), TP),
            P(("groups", "dp"), None),
            P(),
        ),
        out_specs=(
            P(("groups", "dp"), TP),
            P(("groups", "dp"), TP),
            P(("groups", "dp"), TP, None),
            P(("groups", "dp"), None, TP),
        ),
        check_vma=False,
    )
```

```python
import functools

import jax
import jax.numpy as jnp
from jax import lax
from jax.experimental import pallas as pl
from jax.experimental.pallas import tpu as pltpu
from jax.sharding import PartitionSpec as P

adapter_scale = 2.0
TP = ("tensor", "pipe")


def dot(a, b, dims):
    return lax.dot_general(a, b, (dims, ((), ())), preferred_element_type=jnp.float32)


def plain(acts, weight, down, up, dy, token_adapter, adapter_slot):
    per, feat, rank = down.shape
    cols = up.shape[2]
    tok = acts.shape[0]
    adapters = adapter_slot.shape[0]
    wide = adapters * rank
    fold = 2 * rank
    ids = token_adapter[:, 0]
    chosen = ids[:, None] == jnp.arange(adapters, dtype=jnp.int32)[None, :]
    slot_tok = jnp.sum(jnp.where(chosen, adapter_slot[None, :], 0), axis=1)
    slot_hot = slot_tok[:, None] == jnp.arange(adapters, dtype=jnp.int32)[None, :]
    counts = lax.psum(jnp.sum(slot_hot.astype(jnp.float32), axis=0), "dp")
    first = lax.axis_index("dp") * per
    own_counts = lax.dynamic_slice(counts, (first,), (per,))
    mask = slot_tok[:, None] == jnp.arange(wide, dtype=jnp.int32)[None, :] // rank

    def squeeze(full):
        full = jnp.where(mask, full, 0.0)
        return sum(full[:, i : i + fold] for i in range(0, wide, fold))

    def spread(rows):
        return jnp.where(mask, jnp.tile(rows, (1, wide // fold)), 0).astype(jnp.bfloat16)

    up_all = lax.all_gather(up.reshape(per * rank, cols), "dp", axis=0, tiled=True)
    down_all = lax.all_gather(
        down.transpose(1, 0, 2).reshape(feat, per * rank), "dp", axis=1, tiled=True
    )
    weight_all = lax.all_gather(weight, "dp", axis=1, tiled=True)
    dy_all = lax.all_gather(dy, TP, axis=1, tiled=True)

    grad_low = squeeze(dot(dy, up_all, ((1,), (1,)))).astype(jnp.bfloat16)
    grad_low = lax.psum(grad_low, TP).astype(jnp.float32) * adapter_scale
    grad_low = spread(grad_low.astype(jnp.bfloat16))
    part_down = dot(grad_low, acts, ((0,), (0,))).astype(jnp.bfloat16)
    sum_down = lax.psum_scatter(part_down, "dp", scatter_dimension=0, tiled=True)

    low = squeeze(dot(acts, down_all, ((1,), (0,)))).astype(jnp.bfloat16)
    low = spread(lax.psum(low, TP))
    part_up = dot(low, dy, ((0,), (0,))).astype(jnp.bfloat16)
    sum_up = lax.psum_scatter(part_up, "dp", scatter_dimension=0, tiled=True)
    delta = adapter_scale * dot(low, up_all, ((1,), (0,)))

    base = dot(acts, weight_all, ((1,), (0,))).astype(jnp.bfloat16)
    base = lax.psum_scatter(base, TP, scatter_dimension=1, tiled=True)
    layer_out = (base.astype(jnp.float32) + delta).astype(jnp.bfloat16)
    input_gradient = (
        dot(dy_all, weight_all, ((1,), (1,))) + dot(grad_low, down_all, ((1,), (1,)))
    ).astype(jnp.bfloat16)
    grad_down = sum_down.astype(jnp.float32).reshape(per, rank, feat).transpose(0, 2, 1)
    grad_down = grad_down * (1.0 / own_counts)[:, None, None]
    grad_up = sum_up.astype(jnp.float32).reshape(per, rank, cols)
    grad_up = grad_up * (adapter_scale / own_counts)[:, None, None]
    return (layer_out, input_gradient, grad_down, grad_up)


LANES = 128
ROWS = 256


def fused_kernel(
    sizes,
    x_hbm, a_hbm, w_hbm, b_hbm, dy_hbm, slot_col, slot_row, cnt_ref,
    out_ref, ig_ref, down_ref, up_ref, cnt_out,
    x, a_all, w_all, b_all, dy_all, part, recv_r, recv_l, base_send, base_recv, acc,
    fold, grad_low, low, grad_t, lhs, gpack_send, gpack_recv, lpack_send, lpack_recv,
    up_send, up_recv, cnt_recv,
    load_sem, b_ss, b_rs, c_ss, c_rs, az_ss, az_rs, ay_ss, ay_rs, wz_ss, wz_rs, wy_ss, wy_rs,
    dy_ss, dy_rs, g_ss, g_rs, l_ss, l_rs, rs_ss, rr_rs, rl_rs, base_ss, base_rs, up_ss, up_rs,
):
    depth, pipes, peers, per, rank = sizes
    tok, feat = x.shape
    wide = per * rank
    pieces = wide // LANES
    each = LANES // rank
    i = lax.axis_index("dp")
    g = lax.axis_index("groups")
    k = lax.axis_index("tensor") * pipes + lax.axis_index("pipe")
    half = feat // 2
    mine = pl.ds(pl.multiple_of(g * half, half), half)
    other = pl.ds(pl.multiple_of((1 - g) * half, half), half)
    y_dev = {"groups": 1 - g}

    def tp_dev(kk):
        return {"tensor": kk // pipes, "pipe": kk % pipes}

    def rc(src, dst, ss, rs, dev):
        return pltpu.make_async_remote_copy(
            src_ref=src, dst_ref=dst, send_sem=ss, recv_sem=rs,
            device_id=dev, device_id_type=pl.DeviceIdType.MESH,
        )

    loads = [
        pltpu.make_async_copy(b_hbm, b_all.at[i], load_sem.at[0]),
        pltpu.make_async_copy(a_hbm, a_all.at[i], load_sem.at[1]),
        pltpu.make_async_copy(x_hbm, x, load_sem.at[2]),
        pltpu.make_async_copy(w_hbm, w_all.at[i], load_sem.at[3]),
        pltpu.make_async_copy(dy_hbm, dy_all.at[k], load_sem.at[4]),
    ]
    for c in loads:
        c.start()

    barrier = pltpu.get_barrier_semaphore()
    for q in range(1, depth):
        pl.semaphore_signal(barrier, inc=1, device_id={"dp": (i + q) % depth},
                            device_id_type=pl.DeviceIdType.MESH)
    for q in range(1, peers):
        pl.semaphore_signal(barrier, inc=1, device_id=tp_dev((k + q) % peers),
                            device_id_type=pl.DeviceIdType.MESH)
    pl.semaphore_signal(barrier, inc=1, device_id=y_dev, device_id_type=pl.DeviceIdType.MESH)
    pl.semaphore_wait(barrier, depth + peers - 1)

    def b_copy(j, src):
        return rc(b_all.at[src], b_all.at[src], b_ss.at[j], b_rs.at[src], {"dp": j})

    def c_copy(j, src):
        return rc(cnt_ref.at[j], cnt_recv.at[src], c_ss.at[j], c_rs.at[src], {"dp": j})

    def tp_copy(send, recv, ss, rs, kk, src):
        return rc(send, recv.at[src], ss.at[kk], rs.at[src], tp_dev(kk))

    def dy_copy(kk, src):
        return rc(dy_all.at[src], dy_all.at[src], dy_ss.at[kk], dy_rs.at[src], tp_dev(kk))

    def z_copy(buf, ss, rs, src, way, to):
        ref = buf.at[src, mine]
        return rc(ref, ref, ss.at[way, src], rs.at[src], {"dp": to})

    def y_copy(buf, ss, rs, src, rows):
        ref = buf.at[src, rows]
        return rc(ref, ref, ss.at[src], rs.at[src], y_dev)

    def own_sends(buf, ss, rs):
        @pl.when(i > 0)
        def _():
            z_copy(buf, ss, rs, i, 1, i - 1).start()

        @pl.when(i < depth - 1)
        def _():
            z_copy(buf, ss, rs, i, 0, i + 1).start()

    def ways(s, body):
        def step(way, carry):
            src = i + (2 * way - 1) * s

            @pl.when((src >= 0) & (src < depth))
            def _():
                body(src, way)

            return carry

        lax.fori_loop(0, 2, step, 0)

    def forward(buf, zs, zr, ys, yr, s):
        def body(src, way):
            to = i + 1 - 2 * way
            z_copy(buf, zs, zr, src, way, (i + 1) % depth).wait_recv()

            @pl.when((to >= 0) & (to < depth))
            def _():
                z_copy(buf, zs, zr, src, way, to).start()

            y_copy(buf, ys, yr, src, mine).start()

        ways(s, body)

    def drain(buf, zs, zr, ys, yr):
        @pl.when(i > 0)
        def _():
            z_copy(buf, zs, zr, i, 1, i - 1).wait_send()

        @pl.when(i < depth - 1)
        def _():
            z_copy(buf, zs, zr, i, 0, i + 1).wait_send()

        for s in range(1, depth):

            def body(src, way):
                to = i + 1 - 2 * way

                @pl.when((to >= 0) & (to < depth))
                def _():
                    z_copy(buf, zs, zr, src, way, to).wait_send()

                y_copy(buf, ys, yr, src, mine).wait_send()

            ways(s, body)

    lane_slot = lax.broadcasted_iota(jnp.int32, (ROWS, LANES), 1) // rank
    low_lanes = lax.broadcasted_iota(jnp.int32, (tok // 2, LANES), 1) < LANES // 2

    def tiles(n, body):
        def step(t, carry):
            body(t)
            return carry

        lax.fori_loop(0, n, step, 0)

    def rows_at(t, size=ROWS):
        return pl.ds(pl.multiple_of(t * size, size), size)

    def folded(z, j, rows):
        total = None
        for p in range(pieces):
            hit = slot_col[rows, :] == lane_slot + (per * j + each * p)
            term = jnp.where(hit, z[:, p * LANES : (p + 1) * LANES], 0.0)
            total = term if total is None else total + term
        return total

    def spread(values, j, rows):
        v = values[rows, :]
        out = [
            jnp.where(slot_col[rows, :] == lane_slot + (per * j + each * p), v, 0.0)
            for p in range(pieces)
        ]
        return jnp.concatenate(out, axis=1).astype(jnp.bfloat16)

    def transposed(values_t, j):
        for p in range(pieces):
            row_slot = lax.broadcasted_iota(jnp.int32, (LANES, tok), 0) // rank
            hit = slot_row[0:1, :] == row_slot + (per * j + each * p)
            lhs[p * LANES : (p + 1) * LANES, :] = jnp.where(hit, values_t[...], 0.0).astype(
                jnp.bfloat16
            )

    def pack(dst):
        f = fold[...]
        f = f + pltpu.roll(f, LANES // 2, 1)
        dst[...] = jnp.where(low_lanes, f[: tok // 2], f[tok // 2 :]).astype(jnp.bfloat16)

    def unpack(send, recv, ss, rs, dst, scale):
        total = send[...].astype(jnp.float32)
        for q in range(1, peers):
            kk = (k + q) % peers
            tp_copy(send, recv, ss, rs, kk, kk).wait_recv()
            total = total + recv[kk].astype(jnp.float32)
        total = (scale * total).astype(jnp.bfloat16).astype(jnp.float32)
        turned = pltpu.roll(total, LANES // 2, 1)
        dst[: tok // 2, :] = jnp.where(low_lanes, total, turned)
        dst[tok // 2 :, :] = jnp.where(low_lanes, turned, total)

    def low_add(j):
        def body(t):
            rows = rows_at(t)
            z = dot(x[rows, :], a_all[j], ((1,), (0,)))
            fold[rows, :] = fold[rows, :] + folded(z, j, rows)

        tiles(tok // ROWS, body)

    def base_block(j):
        def body(t):
            rows = rows_at(t)
            base_send[j, rows, :] = dot(x[rows, :], w_all[j], ((1,), (0,))).astype(jnp.bfloat16)

        tiles(tok // ROWS, body)

        @pl.when(j != k)
        def _():
            base_copy(j, k).start()

    def base_copy(j, src):
        return rc(base_send.at[j], base_recv.at[src], base_ss.at[j], base_rs.at[src], tp_dev(j))

    wide_cols = 512

    def back_a(j, first):
        def body(t):
            rows = rows_at(t)
            left = spread(grad_low, j, rows)

            def inner(c):
                cols = rows_at(c, wide_cols)
                z = dot(left, a_all[j, cols, :], ((1,), (1,)))
                acc[rows, cols] = z if first else acc[rows, cols] + z

            tiles(feat // wide_cols, inner)

        tiles(tok // ROWS, body)

    def back_w(j):
        def body(t):
            rows = rows_at(t)

            def inner(c):
                cols = rows_at(c, wide_cols)
                z = dot(dy_all[j, rows, :], w_all[j, cols, :], ((1,), (1,)))
                acc[rows, cols] = acc[rows, cols] + z

            tiles(feat // wide_cols, inner)

        tiles(tok // ROWS, body)

    def make_part(d, h):
        transposed(grad_t, d)

        def body(c):
            cols = rows_at(c + h * half_tiles, wide_cols)
            part[d, :, cols] = dot(lhs[...], x[:, cols], ((1,), (0,))).astype(jnp.bfloat16)

        tiles(half_tiles, body)

    half_tiles = half // wide_cols

    def add_to_part(d, h, recv):
        def body(c):
            cols = rows_at(c + h * half_tiles, wide_cols)
            total = part[d, :, cols].astype(jnp.float32) + recv[d, :, cols].astype(jnp.float32)
            part[d, :, cols] = total.astype(jnp.bfloat16)

        tiles(half_tiles, body)

    def rs_up(d, h, to):
        at = (d, slice(None), pl.ds(h * half, half))
        return rc(part.at[at], recv_r.at[at], rs_ss.at[h, d], rr_rs.at[h, d], {"dp": to})

    def rs_down(d, h, to):
        at = (d, slice(None), pl.ds(h * half, half))
        return rc(part.at[at], recv_l.at[at], rs_ss.at[h, d], rl_rs.at[h, d], {"dp": to})

    def reduce_step(t, h):
        @pl.when(t >= i)
        def _():
            d = depth - 1 - t + i
            make_part(d, h)

            @pl.when(i > 0)
            def _():
                rs_up(d, h, i + 1).wait_recv()
                add_to_part(d, h, recv_r)

            rs_up(d, h, i + 1).start()

        @pl.when(t >= depth - 1 - i)
        def _():
            d = i - (depth - 1 - t)
            make_part(d, h)

            @pl.when(i < depth - 1)
            def _():
                rs_down(d, h, i - 1).wait_recv()
                add_to_part(d, h, recv_l)

            rs_down(d, h, i - 1).start()

    loads[0].wait()
    for q in range(1, depth):
        b_copy((i + q) % depth, i).start()
    for q in range(1, depth):
        c_copy((i + q) % depth, i).start()
    loads[1].wait()
    own_sends(a_all, az_ss, az_rs)
    loads[2].wait()
    loads[3].wait()
    base_block(i)

    loads[4].wait()
    fold[...] = jnp.zeros_like(fold)

    def grad_low_add(j):
        def body(t):
            rows = rows_at(t)
            z = dot(dy_all[k, rows, :], b_all[j], ((1,), (1,)))
            fold[rows, :] = fold[rows, :] + folded(z, j, rows)

        tiles(tok // ROWS, body)

    grad_low_add(i)

    def b_step(q, carry):
        j = (i + q) % depth
        b_copy(j, j).wait_recv()
        grad_low_add(j)
        return carry

    lax.fori_loop(1, depth, b_step, 0)
    pack(gpack_send)
    for q in range(1, peers):
        tp_copy(gpack_send, gpack_recv, g_ss, g_rs, (k + q) % peers, k).start()
    for q in range(1, peers):
        dy_copy((k + q) % peers, k).start()
    own_sends(w_all, wz_ss, wz_rs)
    fold[...] = jnp.zeros_like(fold)
    low_add(i)
    unpack(gpack_send, gpack_recv, g_ss, g_rs, grad_low, adapter_scale)
    grad_t[...] = jnp.transpose(grad_low[...])

    def use_a(src, way):
        y_copy(a_all, ay_ss, ay_rs, src, other).wait_recv()
        low_add(src)
        back_a(src, False)

    def forward_a(step):
        forward(a_all, az_ss, az_rs, ay_ss, ay_rs, step)

    def forward_w(step):
        forward(w_all, wz_ss, wz_rs, wy_ss, wy_rs, step)

    last = depth - 1
    reduce_step(0, 0)
    forward_a(1)
    reduce_step(0, 1)
    back_a(i, True)
    for t in range(1, last):
        if t == 1:
            forward_a(2)
        forward_w(t)
        ways(t, use_a)
        reduce_step(t, 0)
        if t + 2 <= last:
            forward_a(t + 2)
        reduce_step(t, 1)
    forward_w(last)
    ways(last, use_a)
    pack(lpack_send)
    for q in range(1, peers):
        tp_copy(lpack_send, lpack_recv, l_ss, l_rs, (k + q) % peers, k).start()
    for q in range(1, peers):
        kk = (k + q) % peers
        dy_copy(kk, kk).wait_recv()
    back_w(i)
    unpack(lpack_send, lpack_recv, l_ss, l_rs, low, 1.0)
    grad_t[...] = jnp.transpose(low[...])

    def up_copy(j, src):
        return rc(up_send.at[j], up_recv.at[src], up_ss.at[j], up_rs.at[src], {"dp": j})

    def up_part(q, carry):
        j = (i + q) % depth
        transposed(grad_t, j)
        up_send[j] = dot(lhs[...], dy_all[k], ((1,), (0,))).astype(jnp.bfloat16)

        @pl.when(q < depth)
        def _():
            up_copy(j, i).start()

        return carry

    lax.fori_loop(1, depth + 1, up_part, 0)

    def use_w(src, way):
        y_copy(w_all, wy_ss, wy_rs, src, other).wait_recv()
        base_block(src)
        back_w(src)

    for step in range(1, last):
        ways(step, use_w)

    grad_t[...] = jnp.transpose(grad_low[...])
    for h in range(2):
        make_part(i, h)

        @pl.when(i > 0)
        def _():
            rs_up(i, h, (i + 1) % depth).wait_recv()
            add_to_part(i, h, recv_r)

        @pl.when(i < depth - 1)
        def _():
            rs_down(i, h, (i + 1) % depth).wait_recv()
            add_to_part(i, h, recv_l)

    def down_out(c):
        cols = rows_at(c, wide_cols)
        down_ref[:, cols] = part[i, :, cols].astype(jnp.float32)

    tiles(feat // wide_cols, down_out)

    ways(depth - 1, use_w)

    total = up_send[i].astype(jnp.float32)
    cnt = cnt_ref[i]
    for q in range(1, depth):
        j = (i + q) % depth
        up_copy(j, j).wait_recv()
        total = total + up_recv[j].astype(jnp.float32)
        c_copy(j, j).wait_recv()
        cnt = cnt + cnt_recv[j]
    up_ref[...] = total
    cnt_out[...] = cnt

    def ig_out(t):
        rows = rows_at(t, 64)
        ig_ref[rows, :] = acc[rows, :].astype(jnp.bfloat16)

    tiles(tok // 64, ig_out)

    for q in range(1, peers):
        kk = (k + q) % peers
        base_copy(kk, kk).wait_recv()

    def finish(t):
        rows = rows_at(t)
        delta = None
        for j in range(depth):
            z = dot(spread(low, j, rows), b_all[j], ((1,), (0,)))
            delta = z if delta is None else delta + z
        delta = (adapter_scale * delta).astype(jnp.bfloat16).astype(jnp.float32)
        base = base_send[k, rows, :].astype(jnp.float32)
        for q in range(1, peers):
            base = base + base_recv[(k + q) % peers, rows, :].astype(jnp.float32)
        out_ref[rows, :] = (base + delta).astype(jnp.bfloat16)

    tiles(tok // ROWS, finish)

    drain(a_all, az_ss, az_rs, ay_ss, ay_rs)
    drain(w_all, wz_ss, wz_rs, wy_ss, wy_rs)
    for q in range(1, depth):
        j = (i + q) % depth
        b_copy(j, i).wait_send()
        c_copy(j, i).wait_send()
        up_copy(j, i).wait_send()
        rs_up(j, 0, j).wait_send()
        rs_up(j, 1, j).wait_send()
    for q in range(1, peers):
        kk = (k + q) % peers
        tp_copy(gpack_send, gpack_recv, g_ss, g_rs, kk, k).wait_send()
        tp_copy(lpack_send, lpack_recv, l_ss, l_rs, kk, k).wait_send()
        dy_copy(kk, k).wait_send()
        base_copy(kk, k).wait_send()


def fused(mesh_sizes, acts, weight, down, up, dy, token_adapter, adapter_slot):
    depth, pipes, peers = mesh_sizes
    per, feat, rank = down.shape
    cols = up.shape[2]
    tok = acts.shape[0]
    adapters = adapter_slot.shape[0]
    wide = per * rank
    ids = token_adapter[:, 0]
    everyone = jnp.arange(adapters, dtype=jnp.int32)
    slot_tok = jnp.sum(jnp.where(ids[:, None] == everyone[None, :], adapter_slot[None, :], 0), axis=1)
    counts = jnp.sum((slot_tok[:, None] == everyone[None, :]).astype(jnp.float32), axis=0)
    cnt = jnp.broadcast_to(jnp.repeat(counts, rank).reshape(depth, 1, wide), (depth, 8, wide))
    slot_col = jnp.broadcast_to(slot_tok[:, None], (tok, LANES))
    slot_row = jnp.broadcast_to(slot_tok[None, :], (8, tok))
    a = down.transpose(1, 0, 2).reshape(feat, wide)
    b = up.reshape(wide, cols)
    bf, f32 = jnp.bfloat16, jnp.float32
    dma = pltpu.SemaphoreType.DMA
    vmem = pl.BlockSpec(memory_space=pltpu.VMEM)
    hbm = pl.BlockSpec(memory_space=pl.ANY)
    layer_out, ig, sum_down, sum_up, total = pl.pallas_call(
        functools.partial(fused_kernel, (depth, pipes, peers, per, rank)),
        out_shape=(
            jax.ShapeDtypeStruct((tok, cols), bf),
            jax.ShapeDtypeStruct((tok, feat), bf),
            jax.ShapeDtypeStruct((wide, feat), f32),
            jax.ShapeDtypeStruct((wide, cols), f32),
            jax.ShapeDtypeStruct((8, wide), f32),
        ),
        in_specs=[hbm] * 5 + [vmem] * 3,
        out_specs=(vmem,) * 5,
        scratch_shapes=[
            pltpu.VMEM((tok, feat), bf),
            pltpu.VMEM((depth, feat, wide), bf),
            pltpu.VMEM((depth, feat, cols), bf),
            pltpu.VMEM((depth, wide, cols), bf),
            pltpu.VMEM((peers, tok, cols), bf),
            pltpu.VMEM((depth, wide, feat), bf),
            pltpu.VMEM((depth, wide, feat), bf),
            pltpu.VMEM((depth, wide, feat), bf),
            pltpu.VMEM((peers, tok, cols), bf),
            pltpu.VMEM((peers, tok, cols), bf),
            pltpu.VMEM((tok, feat), f32),
            pltpu.VMEM((tok, LANES), f32),
            pltpu.VMEM((tok, LANES), f32),
            pltpu.VMEM((tok, LANES), f32),
            pltpu.VMEM((LANES, tok), f32),
            pltpu.VMEM((wide, tok), bf),
            pltpu.VMEM((tok // 2, LANES), bf),
            pltpu.VMEM((peers, tok // 2, LANES), bf),
            pltpu.VMEM((tok // 2, LANES), bf),
            pltpu.VMEM((peers, tok // 2, LANES), bf),
            pltpu.VMEM((depth, wide, cols), bf),
            pltpu.VMEM((depth, wide, cols), bf),
            pltpu.VMEM((depth, 8, wide), f32),
            dma((5,)),
            dma((depth,)), dma((depth,)), dma((depth,)), dma((depth,)),
            dma((2, depth)), dma((depth,)), dma((depth,)), dma((depth,)),
            dma((2, depth)), dma((depth,)), dma((depth,)), dma((depth,)),
            dma((peers,)), dma((peers,)), dma((peers,)), dma((peers,)),
            dma((peers,)), dma((peers,)),
            dma((2, depth)), dma((2, depth)), dma((2, depth)),
            dma((peers,)), dma((peers,)), dma((depth,)), dma((depth,)),
        ],
        compiler_params=pltpu.CompilerParams(
            collective_id=0, has_side_effects=True, vmem_limit_bytes=60 * 1024 * 1024
        ),
    )(acts, a, weight, b, dy, slot_col, slot_row, cnt)
    own = total[0].reshape(per, rank)[:, 0]
    grad_down = sum_down.reshape(per, rank, feat).transpose(0, 2, 1)
    grad_down = grad_down * (1.0 / own)[:, None, None]
    grad_up = sum_up.reshape(per, rank, cols) * (adapter_scale / own)[:, None, None]
    return (layer_out, ig, grad_down, grad_up)


def local(mesh_sizes, groups, *args):
    acts, weight, down, up, dy, _, adapter_slot = args
    depth, pipes, peers = mesh_sizes
    per, feat, rank = down.shape
    tok, cols = dy.shape
    fits = (
        groups == 2 and depth == peers and LANES == 2 * rank and per * rank % LANES == 0
        and cols % LANES == 0 and weight.shape[1] == cols and tok % 512 == 0
        and feat % 1024 == 0 and per * rank <= 256 and cols <= 256 and tok * feat <= 1 << 21
        and depth <= 4
    )
    if fits:
        return fused(mesh_sizes, *args)
    return plain(*args)


def solution(mesh):
    shape = mesh.shape
    sizes = (shape["dp"], shape["pipe"], shape["tensor"] * shape["pipe"])
    return jax.shard_map(
        functools.partial(local, sizes, shape["groups"]),
        mesh=mesh,
        in_specs=(
            P(("groups", "dp"), TP),
            P(TP, "dp"),
            P("dp", TP, None),
            P("dp", None, TP),
            P(("groups", "dp"), TP),
            P(("groups", "dp"), None),
            P(),
        ),
        out_specs=(
            P(("groups", "dp"), TP),
            P(("groups", "dp"), TP),
            P(("groups", "dp"), TP, None),
            P(("groups", "dp"), None, TP),
        ),
        check_vma=False,
    )
```
